32 devices in a mesh: groups: 2 (over x), row: 4 (over y, core), col: 4 (over z).
Axes of the slice: x: 2, y: 2, z: 4, core: 2. Of those that a mesh axis runs over, the one named last changes fastest.
Arguments:
- vectors: bfloat16 [64, 64, 256], P(('groups', 'row', 'col')), parts along dimension 0, may hold values from -6 to 6
- slot_cluster: int32 [64], P('groups'), parts along dimension 0, may hold values from 0 to 31, as said below
- self_blocks: bfloat16 [64, 256, 256], P(('groups', 'row', 'col')), parts along dimension 0, may hold values from -0.375 to 0.375
- near_blocks: bfloat16 [1536, 256, 256], P(('groups', 'row', 'col')), parts along dimension 0, may hold values from -0.078125 to 0.078125
- adjacent_group_couples: int32 [1536, 2], P(('groups', 'row', 'col')), parts along dimension 0, may hold values from 0 to 31, as said below
- near_count: int32 [32], P(('groups', 'row', 'col')), parts along dimension 0, may hold values from 1 to 48, as said below
- far_left: bfloat16 [4096, 32, 256], P(('groups', 'row', 'col')), parts along dimension 0, may hold values from -0.125 to 0.125
- far_right: bfloat16 [4096, 32, 256], P(('groups', 'row', 'col')), parts along dimension 0, may hold values from -0.375 to 0.375
- distant_group_couples: int32 [4096, 2], P(('groups', 'row', 'col')), parts along dimension 0, may hold values from 0 to 31, as said below
- distant_active_number: int32 [32], P(('groups', 'row', 'col')), parts along dimension 0, may hold values from 1 to 128, as said below
Outputs:
- basis: bfloat16 [3, 64, 64, 256], P(None, ('groups', 'row', 'col')), parts along dimension 1
The draws below stay inside these ranges and needn't reach their ends.
There are 2 independent parts, one for each index of `groups`. The reference program is written for one: setup_inputs(seed, part) draws one part's arguments, and reference() takes and returns one part's arrays. A program takes and returns all parts, laid end to end along the dimension named above; each array names one. Nothing has to cross between parts.
Inputs may be any that keep to these rules, and one draw needn't show every extreme that they name: `slot_cluster`: A permutation of the cluster ids; slot s lies on device s // 2 of the group, devices numbered grid row times the col axis's size plus grid column. `adjacent_group_couples`: entries 48 q to 48 q + 47 belong to device q of the group; their first cluster is held by a device of q's grid row and their second by a device of q's grid column, padding entries included. `distant_group_couples`: entries 128 q to 128 q + 127 belong to device q of the group; their first cluster is held by a device of q's grid row and their second by a device of q's grid column, padding entries included. `near_count`: some device of every draw has all 48 slots live. `distant_active_number`: some device of every draw has all 128 slots live.
All inputs are finite; a program needn't handle non-finite values.
Results may differ from the reference program's by a relative error of at most 0.0055.
Values may be sent and summed in bfloat16 or wider, within the bound.
A program may use at most 128 MiB of HBM per device.

```python
import jax
import jax.numpy as jnp
from jax import lax

LEAF = 256
NRHS = 64
RANK = 32
ITERS = 3
CL_DEV = 2
NEAR_DEV = 48
FAR_DEV = 128
GRID = 16
CLUSTERS = 32
ROW_SPAN = 8
COL_SPAN = 8
NEAR_ALL = 768
FAR_ALL = 2048


def shared_order(key):
    return jax.random.permutation(jax.random.fold_in(key, 101), CLUSTERS).astype(jnp.int32)


def pair_list(key, order, per_device):
    total = GRID * per_device
    device = jnp.arange(total, dtype=jnp.int32) // per_device
    columns = ROW_SPAN // CL_DEV
    grid_row = device // columns
    grid_col = device % columns
    first_key, second_key = jax.random.split(key)
    within_row = jax.random.randint(first_key, (total,), 0, ROW_SPAN, dtype=jnp.int32)
    within_col = jax.random.randint(second_key, (total,), 0, COL_SPAN, dtype=jnp.int32)
    row_slot = grid_row * ROW_SPAN + within_row
    col_slot = (within_col // CL_DEV * columns + grid_col) * CL_DEV + within_col % CL_DEV
    return jnp.stack([order[row_slot], order[col_slot]], axis=-1)


def live_counts(key, per_device, lowest):
    first_key, second_key = jax.random.split(key)
    counts = jax.random.randint(first_key, (GRID,), lowest, per_device + 1, dtype=jnp.int32)
    busiest = jax.random.randint(second_key, (), 0, GRID, dtype=jnp.int32)
    return counts.at[busiest].set(per_device)


def draw_slot_cluster(key, part):
    return shared_order(key)


def draw_adjacent_group_couples(key, part):
    order = shared_order(key)
    key = jax.random.fold_in(key, 3)
    return pair_list(key, order, NEAR_DEV)


def draw_distant_group_couples(key, part):
    order = shared_order(key)
    key = jax.random.fold_in(key, 4)
    return pair_list(key, order, FAR_DEV)


def draw_near_count(key, part):
    key = jax.random.fold_in(key, 5)
    return live_counts(key, NEAR_DEV, max(1, NEAR_DEV // 8))


def draw_distant_active_number(key, part):
    key = jax.random.fold_in(key, 6)
    return live_counts(key, FAR_DEV, max(1, FAR_DEV // 4))


def steps_of(stream_key, extent, cuts, least, largest):
    gain = 1.0
    for dim, blocks in cuts:
        heights = jax.random.uniform(jax.random.fold_in(jax.random.fold_in(stream_key, 6), dim), (blocks,), jnp.float32, least / len(cuts), largest / len(cuts))
        gain = gain * jnp.repeat(jnp.exp(heights), extent[dim] // blocks).reshape((-1,) + (1,) * (len(extent) - 1 - dim))
    return gain


def bell_draw(own_key, extent, deviation, limit, pieces=(), kind=jnp.bfloat16):
    loudness = steps_of(own_key, extent, pieces, -0.22, 0.18) if pieces else 1.0
    array = jax.random.normal(own_key, extent, jnp.float32) * deviation * loudness
    return jnp.minimum(jnp.maximum(array, -limit), limit).astype(kind)


def setup_inputs(seed: int = 0, part: int = 0) -> dict:
    splits = jax.random.split(jax.random.key(seed), 11)
    part_splits = jax.random.split(jax.random.fold_in(splits[10], part), 11)
    return {
        "vectors": bell_draw(part_splits[0], (CLUSTERS, NRHS, LEAF), 1.0, 6.0, ((0, 16),)),
        "slot_cluster": draw_slot_cluster(jax.random.fold_in(jax.random.fold_in(splits[10], part), 71), part),
        "self_blocks": bell_draw(part_splits[2], (CLUSTERS, LEAF, LEAF), LEAF ** -0.5, 0.375, ((0, 16),)),
        "near_blocks": bell_draw(part_splits[3], (NEAR_ALL, LEAF, LEAF), (24 * LEAF) ** -0.5, 0.078125, ((0, 16),)),
        "adjacent_group_couples": draw_adjacent_group_couples(jax.random.fold_in(jax.random.fold_in(splits[10], part), 71), part),
        "near_count": draw_near_count(jax.random.fold_in(jax.random.fold_in(splits[10], part), 71), part),
        "far_left": bell_draw(part_splits[6], (FAR_ALL, RANK, LEAF), (10 * LEAF) ** -0.5, 0.125, ((0, 16),)),
        "far_right": bell_draw(part_splits[7], (FAR_ALL, RANK, LEAF), LEAF ** -0.5, 0.375, ((0, 16),)),
        "distant_group_couples": draw_distant_group_couples(jax.random.fold_in(jax.random.fold_in(splits[10], part), 71), part),
        "distant_active_number": draw_distant_active_number(jax.random.fold_in(jax.random.fold_in(splits[10], part), 71), part),
    }


def live_mask(counts, per_device, total):
    position = jnp.arange(total, dtype=jnp.int32)
    return (position % per_device < jnp.repeat(counts, per_device)).astype(jnp.float32)


def reference(vectors, slot_cluster, self_blocks, near_blocks, adjacent_group_couples, near_count, far_left, far_right, distant_group_couples, distant_active_number):
    slot_of = jnp.zeros((CLUSTERS,), jnp.int32).at[slot_cluster].set(jnp.arange(CLUSTERS, dtype=jnp.int32))
    near_slots = slot_of[adjacent_group_couples].reshape(GRID, NEAR_DEV, 2)
    far_slots = slot_of[distant_group_couples].reshape(GRID, FAR_DEV, 2)
    adjacent_active_markers = live_mask(near_count, NEAR_DEV, NEAR_ALL).reshape(GRID, NEAR_DEV)
    far_live = live_mask(distant_active_number, FAR_DEV, FAR_ALL).reshape(GRID, FAR_DEV)
    near_group = near_blocks.reshape(GRID, NEAR_DEV, LEAF, LEAF)
    left_group = far_left.reshape(GRID, FAR_DEV, RANK, LEAF)
    right_group = far_right.reshape(GRID, FAR_DEV, RANK, LEAF)

    def operator(current):
        wide = current.astype(jnp.float32)
        potential = jnp.einsum('cab,cnb->cna', self_blocks.astype(jnp.float32), wide)

        def near_step(total, item):
            blocks, slots, weight = item
            blocks = blocks.astype(jnp.float32)
            weight = weight[:, None, None]
            forward = jnp.einsum('pab,pnb->pna', blocks, wide[slots[:, 1]]) * weight
            backward = jnp.einsum('pab,pna->pnb', blocks, wide[slots[:, 0]]) * weight
            total = total.at[slots[:, 0]].add(forward)
            total = total.at[slots[:, 1]].add(backward)
            return total, None

        potential, unused = lax.scan(near_step, potential, (near_group, near_slots, adjacent_active_markers))

        def far_step(total, item):
            left, right, slots, weight = item
            left = left.astype(jnp.float32)
            right = right.astype(jnp.float32)
            weight = weight[:, None, None]
            coef_fwd = jnp.einsum('pkb,pnb->pnk', right, wide[slots[:, 1]]).astype(jnp.bfloat16)
            coef_back = jnp.einsum('pka,pna->pnk', left, wide[slots[:, 0]]).astype(jnp.bfloat16)
            coef_fwd = lax.optimization_barrier(coef_fwd).astype(jnp.float32)
            coef_back = lax.optimization_barrier(coef_back).astype(jnp.float32)
            forward = jnp.einsum('pka,pnk->pna', left, coef_fwd) * weight
            backward = jnp.einsum('pkb,pnk->pnb', right, coef_back) * weight
            total = total.at[slots[:, 0]].add(forward)
            total = total.at[slots[:, 1]].add(backward)
            return total, None

        potential, unused = lax.scan(far_step, potential, (left_group, right_group, far_slots, far_live))
        return potential.astype(jnp.bfloat16)

    current = vectors
    powers = []
    for step in range(ITERS):
        current = operator(current)
        powers.append(current)
    return jnp.stack(powers)
```

```python
import functools

import jax
import jax.numpy as jnp
from jax import lax
from jax.experimental import pallas as pl
from jax.experimental.pallas import tpu as pltpu
from jax.sharding import PartitionSpec as P

ITERS = 3
NEAR_FAST = 2
FAR_FAST = 6
DENSE_LIMIT = 16 << 20
MESH = pl.DeviceIdType.MESH


def build_kernel(
    local,
    rows,
    cols,
    slot_cluster,
    near_pairs,
    near_count,
    far_pairs,
    far_count,
    near_hbm,
    left_hbm,
    right_hbm,
    dense,
    near,
    left,
    right,
    total,
    slot_of,
    near_head,
    near_next,
    near_size,
    far_head,
    far_next,
    far_size,
    sems,
):
    near_all, leaf, _ = near_hbm.shape
    far_all, rank, _ = left_hbm.shape
    step = pl.program_id(0)

    @pl.when(step == 0)
    def _():
        copies = [
            pltpu.make_async_copy(left_hbm, left.at[pl.ds(0, far_all)], sems.at[0]),
            pltpu.make_async_copy(right_hbm, right.at[pl.ds(0, far_all)], sems.at[1]),
            pltpu.make_async_copy(near_hbm, near.at[pl.ds(0, near_all)], sems.at[2]),
        ]
        for copy in copies:
            copy.start()
        near[near_all] = jnp.zeros((leaf, leaf), near.dtype)
        left[far_all] = jnp.zeros((rank, leaf), left.dtype)
        right[far_all] = jnp.zeros((rank, leaf), right.dtype)
        grid_row = lax.axis_index("row")
        col_devices = rows // local

        def place_cluster(s, _):
            slot_of[slot_cluster[s]] = s
            return 0

        lax.fori_loop(0, slot_cluster.shape[0], place_cluster, 0)

        def clear(cell, _):
            near_head[cell] = near_all
            near_size[cell] = 0
            far_head[cell] = far_all
            far_size[cell] = 0
            return 0

        lax.fori_loop(0, rows * cols, clear, 0)
        near_next[near_all] = near_all
        far_next[far_all] = far_all

        def chain(pairs, head, following, size):
            def insert(e, _):
                first = slot_of[pairs[0, e]]
                second = slot_of[pairs[1, e]]
                row = first - grid_row * rows
                owner = lax.div(second, local)
                col = lax.div(owner, col_devices) * local + lax.rem(second, local)
                cell = row * cols + col
                following[e] = head[cell]
                head[cell] = e
                size[cell] = size[cell] + 1
                return 0

            return insert

        lax.fori_loop(0, near_count[0], chain(near_pairs, near_head, near_next, near_size), 0)
        lax.fori_loop(0, far_count[0], chain(far_pairs, far_head, far_next, far_size), 0)
        for copy in copies:
            copy.wait()

    def outer(a, b):
        return lax.dot_general(a, b, (((0,), (0,)), ((), ())), preferred_element_type=jnp.float32)

    def one_cell(col):
        cell = step * cols + col
        e = far_head[cell]
        lefts, rights = [], []
        for _ in range(FAR_FAST):
            lefts.append(left[e])
            rights.append(right[e])
            e = far_next[e]
        acc = outer(jnp.concatenate(lefts, axis=0), jnp.concatenate(rights, axis=0))
        e = near_head[cell]
        for _ in range(NEAR_FAST):
            acc = acc + near[e].astype(jnp.float32)
            e = near_next[e]
        dense[:, col * leaf : (col + 1) * leaf] = acc.astype(dense.dtype)

    def long_cell(col):
        cell = step * cols + col

        @pl.when((far_size[cell] > FAR_FAST) | (near_size[cell] > NEAR_FAST))
        def _():
            total[...] = jnp.zeros_like(total)

            def add_near(_, e):
                total[...] += near[e].astype(jnp.float32)
                return near_next[e]

            lax.fori_loop(0, near_size[cell], add_near, near_head[cell])

            def add_far(_, e):
                total[...] += outer(left[e], right[e])
                return far_next[e]

            lax.fori_loop(0, far_size[cell], add_far, far_head[cell])
            dense[:, col * leaf : (col + 1) * leaf] = total[...].astype(dense.dtype)

    for col in range(cols):
        one_cell(col)
    for col in range(cols):
        long_cell(col)


def build(local, rows, cols, slot_cluster, near_blocks, near_pairs, near_count, far_left, far_right, far_pairs, far_count):
    near_all, leaf, _ = near_blocks.shape
    far_all, rank, _ = far_left.shape
    smem = pl.BlockSpec(memory_space=pltpu.SMEM)
    hbm = pl.BlockSpec(memory_space=pl.ANY)
    return pl.pallas_call(
        functools.partial(build_kernel, local, rows, cols),
        grid=(rows,),
        out_shape=jax.ShapeDtypeStruct((rows * leaf, cols * leaf), jnp.bfloat16),
        in_specs=[smem] * 5 + [hbm] * 3,
        out_specs=pl.BlockSpec((leaf, cols * leaf), lambda i: (i, 0)),
        scratch_shapes=[
            pltpu.VMEM((near_all + 1, leaf, leaf), jnp.bfloat16),
            pltpu.VMEM((far_all + 1, rank, leaf), jnp.bfloat16),
            pltpu.VMEM((far_all + 1, rank, leaf), jnp.bfloat16),
            pltpu.VMEM((leaf, leaf), jnp.float32),
            pltpu.SMEM((slot_cluster.shape[0],), jnp.int32),
            pltpu.SMEM((rows * cols,), jnp.int32),
            pltpu.SMEM((near_all + 1,), jnp.int32),
            pltpu.SMEM((rows * cols,), jnp.int32),
            pltpu.SMEM((rows * cols,), jnp.int32),
            pltpu.SMEM((far_all + 1,), jnp.int32),
            pltpu.SMEM((rows * cols,), jnp.int32),
            pltpu.SemaphoreType.DMA((3,)),
        ],
        compiler_params=pltpu.CompilerParams(vmem_limit_bytes=40 << 20),
        cost_estimate=pl.CostEstimate(flops=1 << 29, bytes_accessed=19 << 20, transcendentals=0),
        name="build_dense",
    )(slot_cluster, near_pairs.T, near_count, far_pairs.T, far_count, near_blocks, far_left, far_right)


def power_kernel(
    row_devices,
    col_devices,
    vectors,
    self_blocks,
    dense_hbm,
    basis,
    dense,
    row_in,
    col_in,
    row_out,
    col_out,
    row_part,
    col_part,
    acc,
    send_sems,
    recv_sems,
    load_sem,
):
    local, nrhs, leaf = vectors.shape
    width = local * leaf
    g = lax.axis_index("groups")
    r = lax.axis_index("row")
    c = lax.axis_index("col")
    row_peers = [lax.rem(c + d, col_devices) for d in range(col_devices)]
    col_peers = [lax.rem(r + d, row_devices) for d in range(row_devices)]

    load = pltpu.make_async_copy(dense_hbm, dense, load_sem)
    load.start()

    barrier = pltpu.get_barrier_semaphore()
    for d in range(1, col_devices):
        pl.semaphore_signal(barrier, inc=1, device_id=(g, r, row_peers[d]), device_id_type=MESH)
    for d in range(1, row_devices):
        pl.semaphore_signal(barrier, inc=1, device_id=(g, col_peers[d], c), device_id_type=MESH)
    pl.semaphore_wait(barrier, row_devices + col_devices - 2)

    def remote(kind, k, d, source, target, device):
        return pltpu.make_async_remote_copy(
            src_ref=source,
            dst_ref=target,
            send_sem=send_sems.at[kind, k, d],
            recv_sem=recv_sems.at[kind, k, d],
            device_id=device,
            device_id_type=MESH,
        )

    sent = []
    current = vectors
    for k in range(ITERS):
        gathers_col = [
            remote(0, k, d, current, col_in.at[k, d], (g, col_peers[d], c))
            for d in range(1, row_devices)
        ]
        gathers_row = [
            remote(1, k, d, current, row_in.at[k, d], (g, r, row_peers[d]))
            for d in range(1, col_devices)
        ]
        for copy in gathers_col + gathers_row:
            copy.start()
        for s in range(local):
            acc[s] = lax.dot_general(
                current[s], self_blocks[s], (((1,), (1,)), ((), ())), preferred_element_type=jnp.float32
            )
        if k == 0:
            load.wait()
        for copy in gathers_col:
            copy.wait_recv()

        def held(buffer, d):
            source = current if d == 0 else buffer.at[k, d]
            return jnp.concatenate([source[s] for s in range(local)], axis=1)

        scatters = []
        for d in list(range(1, col_devices)) + [0]:
            owner = row_peers[d]
            part = jnp.zeros((nrhs, width), jnp.float32)
            for b in range(row_devices):
                source = lax.rem(r - b + row_devices, row_devices)
                block = dense[
                    pl.ds(pl.multiple_of(owner * width, width), width),
                    pl.ds(pl.multiple_of(source * width, width), width),
                ]
                part = part + lax.dot_general(
                    held(col_in, b), block, (((1,), (1,)), ((), ())), preferred_element_type=jnp.float32
                )
            for s in range(local):
                piece = part[:, s * leaf : (s + 1) * leaf]
                if d == 0:
                    acc[s] += piece
                else:
                    row_out[k, d, s] = piece.astype(row_out.dtype)
            if d != 0:
                copy = remote(2, k, d, row_out.at[k, d], row_part.at[k, d], (g, r, owner))
                copy.start()
                scatters.append(copy)
        for copy in gathers_row:
            copy.wait_recv()
        for d in list(range(1, row_devices)) + [0]:
            owner = col_peers[d]
            part = jnp.zeros((nrhs, width), jnp.float32)
            for b in range(col_devices):
                source = lax.rem(c - b + col_devices, col_devices)
                block = dense[
                    pl.ds(pl.multiple_of(source * width, width), width),
                    pl.ds(pl.multiple_of(owner * width, width), width),
                ]
                part = part + jnp.dot(held(row_in, b), block, preferred_element_type=jnp.float32)
            for s in range(local):
                piece = part[:, s * leaf : (s + 1) * leaf]
                if d == 0:
                    acc[s] += piece
                else:
                    col_out[k, d, s] = piece.astype(col_out.dtype)
            if d != 0:
                copy = remote(3, k, d, col_out.at[k, d], col_part.at[k, d], (g, owner, c))
                copy.start()
                scatters.append(copy)
        for copy in scatters:
            copy.wait_recv()
        total = acc[...]
        for d in range(1, col_devices):
            total = total + row_part[k, d].astype(jnp.float32)
        for d in range(1, row_devices):
            total = total + col_part[k, d].astype(jnp.float32)
        basis[k] = total.astype(basis.dtype)
        current = basis.at[k]
        sent += gathers_col + gathers_row + scatters
    for copy in sent:
        copy.wait_send()


def powers(row_devices, col_devices, vectors, self_blocks, dense):
    local, nrhs, leaf = vectors.shape
    vmem = pl.BlockSpec(memory_space=pltpu.VMEM)
    block = (local, nrhs, leaf)
    most = max(row_devices, col_devices)
    return pl.pallas_call(
        functools.partial(power_kernel, row_devices, col_devices),
        out_shape=jax.ShapeDtypeStruct((ITERS,) + block, jnp.bfloat16),
        in_specs=[vmem, vmem, pl.BlockSpec(memory_space=pl.ANY)],
        out_specs=vmem,
        scratch_shapes=[
            pltpu.VMEM(dense.shape, dense.dtype),
            pltpu.VMEM((ITERS, col_devices) + block, jnp.bfloat16),
            pltpu.VMEM((ITERS, row_devices) + block, jnp.bfloat16),
            pltpu.VMEM((ITERS, col_devices) + block, jnp.bfloat16),
            pltpu.VMEM((ITERS, row_devices) + block, jnp.bfloat16),
            pltpu.VMEM((ITERS, col_devices) + block, jnp.bfloat16),
            pltpu.VMEM((ITERS, row_devices) + block, jnp.bfloat16),
            pltpu.VMEM(block, jnp.float32),
            pltpu.SemaphoreType.DMA((4, ITERS, most)),
            pltpu.SemaphoreType.DMA((4, ITERS, most)),
            pltpu.SemaphoreType.DMA(()),
        ],
        compiler_params=pltpu.CompilerParams(
            collective_id=0, has_side_effects=True, vmem_limit_bytes=40 << 20
        ),
        cost_estimate=pl.CostEstimate(flops=3 << 30, bytes_accessed=9 << 20, transcendentals=0),
        name="powers",
    )(vectors, self_blocks, dense)


def on_device_dense(
    vectors,
    slot_cluster,
    self_blocks,
    near_blocks,
    adjacent_group_couples,
    near_count,
    far_left,
    far_right,
    distant_group_couples,
    distant_active_number,
):
    local = vectors.shape[0]
    row_devices = lax.axis_size("row")
    col_devices = lax.axis_size("col")
    dense = build(
        local,
        local * col_devices,
        local * row_devices,
        slot_cluster,
        near_blocks,
        adjacent_group_couples,
        near_count,
        far_left,
        far_right,
        distant_group_couples,
        distant_active_number,
    )
    return powers(row_devices, col_devices, vectors, self_blocks, dense)


def on_device(
    vectors,
    slot_cluster,
    self_blocks,
    near_blocks,
    adjacent_group_couples,
    near_count,
    far_left,
    far_right,
    distant_group_couples,
    distant_active_number,
):
    local_slots = vectors.shape[0]
    row_devices = lax.axis_size("row")
    col_devices = lax.axis_size("col")
    row_span = local_slots * col_devices
    col_span = local_slots * row_devices
    grid_row = lax.axis_index("row")
    slot_ids = jnp.arange(slot_cluster.shape[0], dtype=jnp.int32)
    shape_tail = vectors.shape[1:]

    def locate(pairs):
        match = pairs[:, :, None] == slot_cluster[None, None, :]
        slots = jnp.sum(jnp.where(match, slot_ids[None, None, :], 0), axis=2)
        row_place = slots[:, 0] - grid_row * row_span
        owner = slots[:, 1] // local_slots
        col_place = owner // col_devices * local_slots + slots[:, 1] % local_slots
        return (row_place, col_place)

    def couple_activity(couple_number, coefficient_numbers):
        return (jnp.arange(coefficient_numbers, dtype=jnp.int32) < couple_number).astype(
            jnp.float32
        )[:, None, None]

    near_rows, near_cols = locate(adjacent_group_couples)
    far_rows, far_cols = locate(distant_group_couples)
    adjacent_active_markers = near_count[0]
    adjacent_couple_selector = couple_activity(
        adjacent_active_markers, adjacent_group_couples.shape[0]
    )
    distant_couple_selector = couple_activity(
        distant_active_number[0], distant_group_couples.shape[0]
    )
    current = vectors
    powers = []
    for step in range(ITERS):
        row_vectors = lax.all_gather(current, "col", axis=0, tiled=True)
        col_vectors = lax.all_gather(current, "row", axis=0, tiled=True)
        own_term = jnp.einsum(
            "cab,cnb->cna", self_blocks, current, preferred_element_type=jnp.float32
        )
        far_first = jnp.take(row_vectors, far_rows, axis=0)
        far_second = jnp.take(col_vectors, far_cols, axis=0)
        coef_fwd = jnp.einsum(
            "pkb,pnb->pnk", far_right, far_second, preferred_element_type=jnp.float32
        ).astype(jnp.bfloat16)
        coef_back = jnp.einsum(
            "pka,pna->pnk", far_left, far_first, preferred_element_type=jnp.float32
        ).astype(jnp.bfloat16)
        far_fwd = (
            jnp.einsum("pka,pnk->pna", far_left, coef_fwd, preferred_element_type=jnp.float32)
            * distant_couple_selector
        )
        far_back = (
            jnp.einsum("pkb,pnk->pnb", far_right, coef_back, preferred_element_type=jnp.float32)
            * distant_couple_selector
        )
        row_total = jnp.zeros((row_span,) + shape_tail, jnp.float32).at[far_rows].add(far_fwd)
        col_total = jnp.zeros((col_span,) + shape_tail, jnp.float32).at[far_cols].add(far_back)
        near_first = jnp.take(row_vectors, near_rows, axis=0)
        near_second = jnp.take(col_vectors, near_cols, axis=0)
        near_fwd = (
            jnp.einsum("pab,pnb->pna", near_blocks, near_second, preferred_element_type=jnp.float32)
            * adjacent_couple_selector
        )
        near_back = (
            jnp.einsum("pab,pna->pnb", near_blocks, near_first, preferred_element_type=jnp.float32)
            * adjacent_couple_selector
        )
        row_total = row_total.at[near_rows].add(near_fwd)
        col_total = col_total.at[near_cols].add(near_back)
        row_share = lax.psum_scatter(row_total, "col", scatter_dimension=0, tiled=True)
        col_share = lax.psum_scatter(col_total, "row", scatter_dimension=0, tiled=True)
        current = (own_term + row_share + col_share).astype(jnp.bfloat16)
        powers.append(current)
    return jnp.stack(powers)


def solution(mesh):
    def program(*args):
        leaf = args[0].shape[2]
        cells = args[0].shape[0] // mesh.shape["groups"]
        cells *= cells // (mesh.shape["row"] * mesh.shape["col"])
        fits = cells * leaf * leaf * 2 <= DENSE_LIMIT
        return mapped(mesh, on_device_dense if fits else on_device)(*args)

    return program


def mapped(mesh, body):
    return jax.shard_map(
        body,
        mesh=mesh,
        in_specs=(
            P(("groups", "row", "col"), None, None),
            P("groups"),
            P(("groups", "row", "col"), None, None),
            P(("groups", "row", "col"), None, None),
            P(("groups", "row", "col"), None),
            P(("groups", "row", "col")),
            P(("groups", "row", "col"), None, None),
            P(("groups", "row", "col"), None, None),
            P(("groups", "row", "col"), None),
            P(("groups", "row", "col")),
        ),
        out_specs=P(None, ("groups", "row", "col"), None, None),
        check_vma=False,
    )
```

```python
import functools

import jax
import jax.numpy as jnp
from jax import lax
from jax.experimental import pallas as pl
from jax.experimental.pallas import tpu as pltpu
from jax.sharding import PartitionSpec as P

ITERS = 3
NEAR_FAST = 2
FAR_FAST = 6
DENSE_LIMIT = 16 << 20
MESH = pl.DeviceIdType.MESH


def build_kernel(
    local,
    rows,
    cols,
    slot_cluster_hbm,
    near_pairs_hbm,
    near_count_hbm,
    far_pairs_hbm,
    far_count_hbm,
    near_hbm,
    left_hbm,
    right_hbm,
    dense,
    slot_cluster,
    near_pairs,
    near_count,
    far_pairs,
    far_count,
    near,
    left,
    right,
    total,
    slot_of,
    near_head,
    near_next,
    near_size,
    far_head,
    far_next,
    far_size,
    sems,
):
    near_all, leaf, _ = near_hbm.shape
    far_all, rank, _ = left_hbm.shape
    step = pl.program_id(0)

    @pl.when(step == 0)
    def _():
        copies = [
            pltpu.make_async_copy(left_hbm, left.at[pl.ds(0, far_all)], sems.at[0]),
            pltpu.make_async_copy(right_hbm, right.at[pl.ds(0, far_all)], sems.at[1]),
            pltpu.make_async_copy(near_hbm, near.at[pl.ds(0, near_all)], sems.at[2]),
        ]
        lists = [
            pltpu.make_async_copy(slot_cluster_hbm, slot_cluster, sems.at[3]),
            pltpu.make_async_copy(near_pairs_hbm, near_pairs, sems.at[4]),
            pltpu.make_async_copy(near_count_hbm, near_count, sems.at[5]),
            pltpu.make_async_copy(far_pairs_hbm, far_pairs, sems.at[6]),
            pltpu.make_async_copy(far_count_hbm, far_count, sems.at[7]),
        ]
        for copy in lists + copies:
            copy.start()
        near[near_all] = jnp.zeros((leaf, leaf), near.dtype)
        left[far_all] = jnp.zeros((rank, leaf), left.dtype)
        right[far_all] = jnp.zeros((rank, leaf), right.dtype)
        grid_row = lax.axis_index("row")
        col_devices = rows // local

        def clear(cell, _):
            near_head[cell] = near_all
            near_size[cell] = 0
            far_head[cell] = far_all
            far_size[cell] = 0
            return 0

        lax.fori_loop(0, rows * cols, clear, 0)
        for copy in lists:
            copy.wait()

        def place_cluster(s, _):
            slot_of[slot_cluster[s]] = s
            return 0

        lax.fori_loop(0, slot_cluster.shape[0], place_cluster, 0)

        near_next[near_all] = near_all
        far_next[far_all] = far_all

        def chain(pairs, head, following, size):
            def insert(e, _):
                first = slot_of[pairs[0, e]]
                second = slot_of[pairs[1, e]]
                row = first - grid_row * rows
                owner = lax.div(second, local)
                col = lax.div(owner, col_devices) * local + lax.rem(second, local)
                cell = row * cols + col
                following[e] = head[cell]
                head[cell] = e
                size[cell] = size[cell] + 1
                return 0

            return insert

        lax.fori_loop(0, near_count[0], chain(near_pairs, near_head, near_next, near_size), 0)
        lax.fori_loop(0, far_count[0], chain(far_pairs, far_head, far_next, far_size), 0)
        for copy in copies:
            copy.wait()

    def outer(a, b):
        return lax.dot_general(a, b, (((0,), (0,)), ((), ())), preferred_element_type=jnp.float32)

    def one_cell(col):
        cell = step * cols + col
        e = far_head[cell]
        lefts, rights = [], []
        for _ in range(FAR_FAST):
            lefts.append(left[e])
            rights.append(right[e])
            e = far_next[e]
        acc = outer(jnp.concatenate(lefts, axis=0), jnp.concatenate(rights, axis=0))
        e = near_head[cell]
        for _ in range(NEAR_FAST):
            acc = acc + near[e].astype(jnp.float32)
            e = near_next[e]
        dense[:, col * leaf : (col + 1) * leaf] = acc.astype(dense.dtype)

    def long_cell(col):
        cell = step * cols + col

        @pl.when((far_size[cell] > FAR_FAST) | (near_size[cell] > NEAR_FAST))
        def _():
            total[...] = jnp.zeros_like(total)

            def add_near(_, e):
                total[...] += near[e].astype(jnp.float32)
                return near_next[e]

            lax.fori_loop(0, near_size[cell], add_near, near_head[cell])

            def add_far(_, e):
                total[...] += outer(left[e], right[e])
                return far_next[e]

            lax.fori_loop(0, far_size[cell], add_far, far_head[cell])
            dense[:, col * leaf : (col + 1) * leaf] = total[...].astype(dense.dtype)

    for col in range(cols):
        one_cell(col)
    for col in range(cols):
        long_cell(col)


def build(local, rows, cols, slot_cluster, near_blocks, near_pairs, near_count, far_left, far_right, far_pairs, far_count):
    near_all, leaf, _ = near_blocks.shape
    far_all, rank, _ = far_left.shape
    hbm = pl.BlockSpec(memory_space=pltpu.HBM)
    return pl.pallas_call(
        functools.partial(build_kernel, local, rows, cols),
        grid=(rows,),
        out_shape=jax.ShapeDtypeStruct((rows * leaf, cols * leaf), jnp.bfloat16),
        in_specs=[hbm] * 8,
        out_specs=pl.BlockSpec((leaf, cols * leaf), lambda i: (i, 0)),
        scratch_shapes=[
            pltpu.SMEM(slot_cluster.shape, jnp.int32),
            pltpu.SMEM((2, near_all), jnp.int32),
            pltpu.SMEM(near_count.shape, jnp.int32),
            pltpu.SMEM((2, far_all), jnp.int32),
            pltpu.SMEM(far_count.shape, jnp.int32),
            pltpu.VMEM((near_all + 1, leaf, leaf), jnp.bfloat16),
            pltpu.VMEM((far_all + 1, rank, leaf), jnp.bfloat16),
            pltpu.VMEM((far_all + 1, rank, leaf), jnp.bfloat16),
            pltpu.VMEM((leaf, leaf), jnp.float32),
            pltpu.SMEM((slot_cluster.shape[0],), jnp.int32),
            pltpu.SMEM((rows * cols,), jnp.int32),
            pltpu.SMEM((near_all + 1,), jnp.int32),
            pltpu.SMEM((rows * cols,), jnp.int32),
            pltpu.SMEM((rows * cols,), jnp.int32),
            pltpu.SMEM((far_all + 1,), jnp.int32),
            pltpu.SMEM((rows * cols,), jnp.int32),
            pltpu.SemaphoreType.DMA((8,)),
        ],
        compiler_params=pltpu.CompilerParams(vmem_limit_bytes=60 << 20),
        cost_estimate=pl.CostEstimate(flops=1 << 29, bytes_accessed=19 << 20, transcendentals=0),
        name="build_dense",
    )(slot_cluster, near_pairs.T, near_count, far_pairs.T, far_count, near_blocks, far_left, far_right)


def power_kernel(
    row_devices,
    col_devices,
    vectors,
    self_blocks,
    dense_hbm,
    basis,
    dense,
    row_in,
    col_in,
    row_out,
    col_out,
    row_part,
    col_part,
    acc,
    send_sems,
    recv_sems,
    load_sem,
):
    local, nrhs, leaf = vectors.shape
    width = local * leaf
    g = lax.axis_index("groups")
    r = lax.axis_index("row")
    c = lax.axis_index("col")
    row_peers = [lax.rem(c + d, col_devices) for d in range(col_devices)]
    col_peers = [lax.rem(r + d, row_devices) for d in range(row_devices)]

    load = pltpu.make_async_copy(dense_hbm, dense, load_sem)
    load.start()

    barrier = pltpu.get_barrier_semaphore()
    for d in range(1, col_devices):
        pl.semaphore_signal(barrier, inc=1, device_id=(g, r, row_peers[d]), device_id_type=MESH)
    for d in range(1, row_devices):
        pl.semaphore_signal(barrier, inc=1, device_id=(g, col_peers[d], c), device_id_type=MESH)
    pl.semaphore_wait(barrier, row_devices + col_devices - 2)

    def remote(kind, k, d, source, target, device):
        return pltpu.make_async_remote_copy(
            src_ref=source,
            dst_ref=target,
            send_sem=send_sems.at[kind, k, d],
            recv_sem=recv_sems.at[kind, k, d],
            device_id=device,
            device_id_type=MESH,
        )

    sent = []
    current = vectors
    for k in range(ITERS):
        gathers_col = [
            remote(0, k, d, current, col_in.at[k, d], (g, col_peers[d], c))
            for d in range(1, row_devices)
        ]
        gathers_row = [
            remote(1, k, d, current, row_in.at[k, d], (g, r, row_peers[d]))
            for d in range(1, col_devices)
        ]
        for copy in gathers_col + gathers_row:
            copy.start()
        for s in range(local):
            acc[s] = lax.dot_general(
                current[s], self_blocks[s], (((1,), (1,)), ((), ())), preferred_element_type=jnp.float32
            )
        if k == 0:
            load.wait()
        for copy in gathers_col:
            copy.wait_recv()

        def held(buffer, d):
            source = current if d == 0 else buffer.at[k, d]
            return jnp.concatenate([source[s] for s in range(local)], axis=1)

        scatters = []
        for d in list(range(1, col_devices)) + [0]:
            owner = row_peers[d]
            part = jnp.zeros((nrhs, width), jnp.float32)
            for b in range(row_devices):
                source = lax.rem(r - b + row_devices, row_devices)
                block = dense[
                    pl.ds(pl.multiple_of(owner * width, width), width),
                    pl.ds(pl.multiple_of(source * width, width), width),
                ]
                part = part + lax.dot_general(
                    held(col_in, b), block, (((1,), (1,)), ((), ())), preferred_element_type=jnp.float32
                )
            for s in range(local):
                piece = part[:, s * leaf : (s + 1) * leaf]
                if d == 0:
                    acc[s] += piece
                else:
                    row_out[k, d, s] = piece.astype(row_out.dtype)
            if d != 0:
                copy = remote(2, k, d, row_out.at[k, d], row_part.at[k, d], (g, r, owner))
                copy.start()
                scatters.append(copy)
        for copy in gathers_row:
            copy.wait_recv()
        for d in list(range(1, row_devices)) + [0]:
            owner = col_peers[d]
            part = jnp.zeros((nrhs, width), jnp.float32)
            for b in range(col_devices):
                source = lax.rem(c - b + col_devices, col_devices)
                block = dense[
                    pl.ds(pl.multiple_of(source * width, width), width),
                    pl.ds(pl.multiple_of(owner * width, width), width),
                ]
                part = part + jnp.dot(held(row_in, b), block, preferred_element_type=jnp.float32)
            for s in range(local):
                piece = part[:, s * leaf : (s + 1) * leaf]
                if d == 0:
                    acc[s] += piece
                else:
                    col_out[k, d, s] = piece.astype(col_out.dtype)
            if d != 0:
                copy = remote(3, k, d, col_out.at[k, d], col_part.at[k, d], (g, owner, c))
                copy.start()
                scatters.append(copy)
        for copy in scatters:
            copy.wait_recv()
        total = acc[...]
        for d in range(1, col_devices):
            total = total + row_part[k, d].astype(jnp.float32)
        for d in range(1, row_devices):
            total = total + col_part[k, d].astype(jnp.float32)
        basis[k] = total.astype(basis.dtype)
        current = basis.at[k]
        sent += gathers_col + gathers_row + scatters
    for copy in sent:
        copy.wait_send()


def powers(row_devices, col_devices, vectors, self_blocks, dense):
    local, nrhs, leaf = vectors.shape
    vmem = pl.BlockSpec(memory_space=pltpu.VMEM)
    block = (local, nrhs, leaf)
    most = max(row_devices, col_devices)
    return pl.pallas_call(
        functools.partial(power_kernel, row_devices, col_devices),
        out_shape=jax.ShapeDtypeStruct((ITERS,) + block, jnp.bfloat16),
        in_specs=[vmem, vmem, pl.BlockSpec(memory_space=pltpu.HBM)],
        out_specs=vmem,
        scratch_shapes=[
            pltpu.VMEM(dense.shape, dense.dtype),
            pltpu.VMEM((ITERS, col_devices) + block, jnp.bfloat16),
            pltpu.VMEM((ITERS, row_devices) + block, jnp.bfloat16),
            pltpu.VMEM((ITERS, col_devices) + block, jnp.bfloat16),
            pltpu.VMEM((ITERS, row_devices) + block, jnp.bfloat16),
            pltpu.VMEM((ITERS, col_devices) + block, jnp.bfloat16),
            pltpu.VMEM((ITERS, row_devices) + block, jnp.bfloat16),
            pltpu.VMEM(block, jnp.float32),
            pltpu.SemaphoreType.DMA((4, ITERS, most)),
            pltpu.SemaphoreType.DMA((4, ITERS, most)),
            pltpu.SemaphoreType.DMA(()),
        ],
        compiler_params=pltpu.CompilerParams(
            collective_id=0, has_side_effects=True, vmem_limit_bytes=57 << 20
        ),
        cost_estimate=pl.CostEstimate(flops=3 << 30, bytes_accessed=9 << 20, transcendentals=0),
        name="powers",
    )(vectors, self_blocks, dense)


def on_device_dense(
    vectors,
    slot_cluster,
    self_blocks,
    near_blocks,
    adjacent_group_couples,
    near_count,
    far_left,
    far_right,
    distant_group_couples,
    distant_active_number,
):
    local = vectors.shape[0]
    row_devices = lax.axis_size("row")
    col_devices = lax.axis_size("col")
    dense = build(
        local,
        local * col_devices,
        local * row_devices,
        slot_cluster,
        near_blocks,
        adjacent_group_couples,
        near_count,
        far_left,
        far_right,
        distant_group_couples,
        distant_active_number,
    )
    return powers(row_devices, col_devices, vectors, self_blocks, dense)


def on_device(
    vectors,
    slot_cluster,
    self_blocks,
    near_blocks,
    adjacent_group_couples,
    near_count,
    far_left,
    far_right,
    distant_group_couples,
    distant_active_number,
):
    local_slots = vectors.shape[0]
    row_devices = lax.axis_size("row")
    col_devices = lax.axis_size("col")
    row_span = local_slots * col_devices
    col_span = local_slots * row_devices
    grid_row = lax.axis_index("row")
    slot_ids = jnp.arange(slot_cluster.shape[0], dtype=jnp.int32)
    shape_tail = vectors.shape[1:]

    def locate(pairs):
        match = pairs[:, :, None] == slot_cluster[None, None, :]
        slots = jnp.sum(jnp.where(match, slot_ids[None, None, :], 0), axis=2)
        row_place = slots[:, 0] - grid_row * row_span
        owner = slots[:, 1] // local_slots
        col_place = owner // col_devices * local_slots + slots[:, 1] % local_slots
        return (row_place, col_place)

    def couple_activity(couple_number, coefficient_numbers):
        return (jnp.arange(coefficient_numbers, dtype=jnp.int32) < couple_number).astype(
            jnp.float32
        )[:, None, None]

    near_rows, near_cols = locate(adjacent_group_couples)
    far_rows, far_cols = locate(distant_group_couples)
    adjacent_active_markers = near_count[0]
    adjacent_couple_selector = couple_activity(
        adjacent_active_markers, adjacent_group_couples.shape[0]
    )
    distant_couple_selector = couple_activity(
        distant_active_number[0], distant_group_couples.shape[0]
    )
    current = vectors
    powers = []
    for step in range(ITERS):
        row_vectors = lax.all_gather(current, "col", axis=0, tiled=True)
        col_vectors = lax.all_gather(current, "row", axis=0, tiled=True)
        own_term = jnp.einsum(
            "cab,cnb->cna", self_blocks, current, preferred_element_type=jnp.float32
        )
        far_first = jnp.take(row_vectors, far_rows, axis=0)
        far_second = jnp.take(col_vectors, far_cols, axis=0)
        coef_fwd = jnp.einsum(
            "pkb,pnb->pnk", far_right, far_second, preferred_element_type=jnp.float32
        ).astype(jnp.bfloat16)
        coef_back = jnp.einsum(
            "pka,pna->pnk", far_left, far_first, preferred_element_type=jnp.float32
        ).astype(jnp.bfloat16)
        far_fwd = (
            jnp.einsum("pka,pnk->pna", far_left, coef_fwd, preferred_element_type=jnp.float32)
            * distant_couple_selector
        )
        far_back = (
            jnp.einsum("pkb,pnk->pnb", far_right, coef_back, preferred_element_type=jnp.float32)
            * distant_couple_selector
        )
        row_total = jnp.zeros((row_span,) + shape_tail, jnp.float32).at[far_rows].add(far_fwd)
        col_total = jnp.zeros((col_span,) + shape_tail, jnp.float32).at[far_cols].add(far_back)
        near_first = jnp.take(row_vectors, near_rows, axis=0)
        near_second = jnp.take(col_vectors, near_cols, axis=0)
        near_fwd = (
            jnp.einsum("pab,pnb->pna", near_blocks, near_second, preferred_element_type=jnp.float32)
            * adjacent_couple_selector
        )
        near_back = (
            jnp.einsum("pab,pna->pnb", near_blocks, near_first, preferred_element_type=jnp.float32)
            * adjacent_couple_selector
        )
        row_total = row_total.at[near_rows].add(near_fwd)
        col_total = col_total.at[near_cols].add(near_back)
        row_share = lax.psum_scatter(row_total, "col", scatter_dimension=0, tiled=True)
        col_share = lax.psum_scatter(col_total, "row", scatter_dimension=0, tiled=True)
        current = (own_term + row_share + col_share).astype(jnp.bfloat16)
        powers.append(current)
    return jnp.stack(powers)


def solution(mesh):
    def program(*args):
        leaf = args[0].shape[2]
        cells = args[0].shape[0] // mesh.shape["groups"]
        cells *= cells // (mesh.shape["row"] * mesh.shape["col"])
        fits = cells * leaf * leaf * 2 <= DENSE_LIMIT
        return mapped(mesh, on_device_dense if fits else on_device)(*args)

    return program


def mapped(mesh, body):
    return jax.shard_map(
        body,
        mesh=mesh,
        in_specs=(
            P(("groups", "row", "col"), None, None),
            P("groups"),
            P(("groups", "row", "col"), None, None),
            P(("groups", "row", "col"), None, None),
            P(("groups", "row", "col"), None),
            P(("groups", "row", "col")),
            P(("groups", "row", "col"), None, None),
            P(("groups", "row", "col"), None, None),
            P(("groups", "row", "col"), None),
            P(("groups", "row", "col")),
        ),
        out_specs=P(None, ("groups", "row", "col"), None, None),
        check_vma=False,
    )
```

```python
import functools

import jax
import jax.numpy as jnp
from jax import lax
from jax.experimental import pallas as pl
from jax.experimental.pallas import tpu as pltpu
from jax.sharding import PartitionSpec as P

ITERS = 3
NEAR_FAST = 3
FAR_FAST = 6
DENSE_LIMIT = 16 << 20
MESH = pl.DeviceIdType.MESH


def build_kernel(
    local,
    rows,
    cols,
    slot_cluster_hbm,
    near_pairs_hbm,
    near_count_hbm,
    far_pairs_hbm,
    far_count_hbm,
    near_hbm,
    left_hbm,
    right_hbm,
    dense,
    slot_cluster,
    near_pairs,
    near_count,
    far_pairs,
    far_count,
    near,
    left,
    right,
    total,
    slot_of,
    near_head,
    near_next,
    near_size,
    far_head,
    far_next,
    far_size,
    sems,
):
    near_all, leaf, _ = near_hbm.shape
    far_all, rank, _ = left_hbm.shape
    step = pl.program_id(0)

    @pl.when(step == 0)
    def _():
        copies = [
            pltpu.make_async_copy(left_hbm, left.at[pl.ds(0, far_all)], sems.at[0]),
            pltpu.make_async_copy(right_hbm, right.at[pl.ds(0, far_all)], sems.at[1]),
            pltpu.make_async_copy(near_hbm, near.at[pl.ds(0, near_all)], sems.at[2]),
        ]
        lists = [
            pltpu.make_async_copy(slot_cluster_hbm, slot_cluster, sems.at[3]),
            pltpu.make_async_copy(near_pairs_hbm, near_pairs, sems.at[4]),
            pltpu.make_async_copy(near_count_hbm, near_count, sems.at[5]),
            pltpu.make_async_copy(far_pairs_hbm, far_pairs, sems.at[6]),
            pltpu.make_async_copy(far_count_hbm, far_count, sems.at[7]),
        ]
        for copy in lists + copies:
            copy.start()
        near[near_all] = jnp.zeros((leaf, leaf), near.dtype)
        left[far_all] = jnp.zeros((rank, leaf), left.dtype)
        right[far_all] = jnp.zeros((rank, leaf), right.dtype)
        grid_row = lax.axis_index("row")
        col_devices = rows // local

        def clear(cell, _):
            near_head[cell] = near_all
            near_size[cell] = 0
            far_head[cell] = far_all
            far_size[cell] = 0
            return 0

        lax.fori_loop(0, rows * cols, clear, 0)
        for copy in lists:
            copy.wait()

        def place_cluster(s, _):
            slot_of[slot_cluster[s]] = s
            return 0

        lax.fori_loop(0, slot_cluster.shape[0], place_cluster, 0)

        near_next[near_all] = near_all
        far_next[far_all] = far_all

        def chain(pairs, head, following, size):
            def insert(e, _):
                first = slot_of[pairs[0, e]]
                second = slot_of[pairs[1, e]]
                row = first - grid_row * rows
                owner = lax.div(second, local)
                col = lax.div(owner, col_devices) * local + lax.rem(second, local)
                cell = row * cols + col
                following[e] = head[cell]
                head[cell] = e
                size[cell] = size[cell] + 1
                return 0

            return insert

        lax.fori_loop(0, near_count[0], chain(near_pairs, near_head, near_next, near_size), 0)
        lax.fori_loop(0, far_count[0], chain(far_pairs, far_head, far_next, far_size), 0)
        for copy in copies:
            copy.wait()

    def outer(a, b):
        return lax.dot_general(a, b, (((0,), (0,)), ((), ())), preferred_element_type=jnp.float32)

    def one_cell(col):
        cell = step * cols + col
        e = far_head[cell]
        lefts, rights = [], []
        for _ in range(FAR_FAST):
            lefts.append(left[e])
            rights.append(right[e])
            e = far_next[e]
        acc = outer(jnp.concatenate(lefts, axis=0), jnp.concatenate(rights, axis=0))
        e = near_head[cell]
        for _ in range(NEAR_FAST):
            acc = acc + near[e].astype(jnp.float32)
            e = near_next[e]
        dense[:, col * leaf : (col + 1) * leaf] = acc.astype(dense.dtype)

    def long_cell(col):
        cell = step * cols + col

        @pl.when((far_size[cell] > FAR_FAST) | (near_size[cell] > NEAR_FAST))
        def _():
            total[...] = jnp.zeros_like(total)

            def add_near(_, e):
                total[...] += near[e].astype(jnp.float32)
                return near_next[e]

            lax.fori_loop(0, near_size[cell], add_near, near_head[cell])

            def add_far(_, e):
                total[...] += outer(left[e], right[e])
                return far_next[e]

            lax.fori_loop(0, far_size[cell], add_far, far_head[cell])
            dense[:, col * leaf : (col + 1) * leaf] = total[...].astype(dense.dtype)

    for col in range(cols):
        one_cell(col)
    for col in range(cols):
        long_cell(col)


def build(local, rows, cols, slot_cluster, near_blocks, near_pairs, near_count, far_left, far_right, far_pairs, far_count):
    near_all, leaf, _ = near_blocks.shape
    far_all, rank, _ = far_left.shape
    hbm = pl.BlockSpec(memory_space=pltpu.HBM)
    return pl.pallas_call(
        functools.partial(build_kernel, local, rows, cols),
        grid=(rows,),
        out_shape=jax.ShapeDtypeStruct((rows * leaf, cols * leaf), jnp.bfloat16),
        in_specs=[hbm] * 8,
        out_specs=pl.BlockSpec((leaf, cols * leaf), lambda i: (i, 0)),
        scratch_shapes=[
            pltpu.SMEM(slot_cluster.shape, jnp.int32),
            pltpu.SMEM((2, near_all), jnp.int32),
            pltpu.SMEM(near_count.shape, jnp.int32),
            pltpu.SMEM((2, far_all), jnp.int32),
            pltpu.SMEM(far_count.shape, jnp.int32),
            pltpu.VMEM((near_all + 1, leaf, leaf), jnp.bfloat16),
            pltpu.VMEM((far_all + 1, rank, leaf), jnp.bfloat16),
            pltpu.VMEM((far_all + 1, rank, leaf), jnp.bfloat16),
            pltpu.VMEM((leaf, leaf), jnp.float32),
            pltpu.SMEM((slot_cluster.shape[0],), jnp.int32),
            pltpu.SMEM((rows * cols,), jnp.int32),
            pltpu.SMEM((near_all + 1,), jnp.int32),
            pltpu.SMEM((rows * cols,), jnp.int32),
            pltpu.SMEM((rows * cols,), jnp.int32),
            pltpu.SMEM((far_all + 1,), jnp.int32),
            pltpu.SMEM((rows * cols,), jnp.int32),
            pltpu.SemaphoreType.DMA((8,)),
        ],
        compiler_params=pltpu.CompilerParams(vmem_limit_bytes=60 << 20),
        cost_estimate=pl.CostEstimate(flops=1 << 29, bytes_accessed=19 << 20, transcendentals=0),
        name="build_dense",
    )(slot_cluster, near_pairs.T, near_count, far_pairs.T, far_count, near_blocks, far_left, far_right)


def power_kernel(
    row_devices,
    col_devices,
    vectors,
    self_blocks,
    dense_hbm,
    basis,
    dense,
    row_in,
    col_in,
    row_out,
    col_out,
    row_part,
    col_part,
    acc,
    send_sems,
    recv_sems,
    load_sem,
):
    local, nrhs, leaf = vectors.shape
    width = local * leaf
    g = lax.axis_index("groups")
    r = lax.axis_index("row")
    c = lax.axis_index("col")
    row_peers = [lax.rem(c + d, col_devices) for d in range(col_devices)]
    col_peers = [lax.rem(r + d, row_devices) for d in range(row_devices)]

    load = pltpu.make_async_copy(dense_hbm, dense, load_sem)
    load.start()

    barrier = pltpu.get_barrier_semaphore()
    for d in range(1, col_devices):
        pl.semaphore_signal(barrier, inc=1, device_id=(g, r, row_peers[d]), device_id_type=MESH)
    for d in range(1, row_devices):
        pl.semaphore_signal(barrier, inc=1, device_id=(g, col_peers[d], c), device_id_type=MESH)
    pl.semaphore_wait(barrier, row_devices + col_devices - 2)

    def remote(kind, k, d, source, target, device):
        return pltpu.make_async_remote_copy(
            src_ref=source,
            dst_ref=target,
            send_sem=send_sems.at[kind, k, d],
            recv_sem=recv_sems.at[kind, k, d],
            device_id=device,
            device_id_type=MESH,
        )

    sent = []
    current = vectors
    for k in range(ITERS):
        gathers_col = [
            remote(0, k, d, current, col_in.at[k, d], (g, col_peers[d], c))
            for d in range(1, row_devices)
        ]
        gathers_row = [
            remote(1, k, d, current, row_in.at[k, d], (g, r, row_peers[d]))
            for d in range(1, col_devices)
        ]
        for copy in gathers_col + gathers_row:
            copy.start()
        for s in range(local):
            acc[s] = lax.dot_general(
                current[s], self_blocks[s], (((1,), (1,)), ((), ())), preferred_element_type=jnp.float32
            )
        if k == 0:
            load.wait()
        for copy in gathers_col:
            copy.wait_recv()

        def held(buffer, d):
            source = current if d == 0 else buffer.at[k, d]
            return jnp.concatenate([source[s] for s in range(local)], axis=1)

        scatters = []
        for d in list(range(1, col_devices)) + [0]:
            owner = row_peers[d]
            part = jnp.zeros((nrhs, width), jnp.float32)
            for b in range(row_devices):
                source = lax.rem(r - b + row_devices, row_devices)
                block = dense[
                    pl.ds(pl.multiple_of(owner * width, width), width),
                    pl.ds(pl.multiple_of(source * width, width), width),
                ]
                part = part + lax.dot_general(
                    held(col_in, b), block, (((1,), (1,)), ((), ())), preferred_element_type=jnp.float32
                )
            for s in range(local):
                piece = part[:, s * leaf : (s + 1) * leaf]
                if d == 0:
                    acc[s] += piece
                else:
                    row_out[k, d, s] = piece.astype(row_out.dtype)
            if d != 0:
                copy = remote(2, k, d, row_out.at[k, d], row_part.at[k, d], (g, r, owner))
                copy.start()
                scatters.append(copy)
        for copy in gathers_row:
            copy.wait_recv()
        near = 1 + 2 * (r % 2)
        for n, d in enumerate([2, row_devices - near, near, 0]):
            owner = lax.rem(r + d, row_devices)
            part = jnp.zeros((nrhs, width), jnp.float32)
            for b in range(col_devices):
                source = lax.rem(c - b + col_devices, col_devices)
                block = dense[
                    pl.ds(pl.multiple_of(source * width, width), width),
                    pl.ds(pl.multiple_of(owner * width, width), width),
                ]
                part = part + jnp.dot(held(row_in, b), block, preferred_element_type=jnp.float32)
            for s in range(local):
                piece = part[:, s * leaf : (s + 1) * leaf]
                if n == 3:
                    acc[s] += piece
                else:
                    col_out[k, d, s] = piece.astype(col_out.dtype)
            if n != 3:
                copy = remote(3, k, d, col_out.at[k, d], col_part.at[k, d], (g, owner, c))
                copy.start()
                scatters.append(copy)
        for copy in scatters:
            copy.wait_recv()
        total = acc[...]
        for d in range(1, col_devices):
            total = total + row_part[k, d].astype(jnp.float32)
        for d in range(1, row_devices):
            total = total + col_part[k, d].astype(jnp.float32)
        basis[k] = total.astype(basis.dtype)
        current = basis.at[k]
        sent += gathers_col + gathers_row + scatters
    for copy in sent:
        copy.wait_send()


def powers(row_devices, col_devices, vectors, self_blocks, dense):
    local, nrhs, leaf = vectors.shape
    vmem = pl.BlockSpec(memory_space=pltpu.VMEM)
    block = (local, nrhs, leaf)
    most = max(row_devices, col_devices)
    return pl.pallas_call(
        functools.partial(power_kernel, row_devices, col_devices),
        out_shape=jax.ShapeDtypeStruct((ITERS,) + block, jnp.bfloat16),
        in_specs=[vmem, vmem, pl.BlockSpec(memory_space=pltpu.HBM)],
        out_specs=vmem,
        scratch_shapes=[
            pltpu.VMEM(dense.shape, dense.dtype),
            pltpu.VMEM((ITERS, col_devices) + block, jnp.bfloat16),
            pltpu.VMEM((ITERS, row_devices) + block, jnp.bfloat16),
            pltpu.VMEM((ITERS, col_devices) + block, jnp.bfloat16),
            pltpu.VMEM((ITERS, row_devices) + block, jnp.bfloat16),
            pltpu.VMEM((ITERS, col_devices) + block, jnp.bfloat16),
            pltpu.VMEM((ITERS, row_devices) + block, jnp.bfloat16),
            pltpu.VMEM(block, jnp.float32),
            pltpu.SemaphoreType.DMA((4, ITERS, most)),
            pltpu.SemaphoreType.DMA((4, ITERS, most)),
            pltpu.SemaphoreType.DMA(()),
        ],
        compiler_params=pltpu.CompilerParams(
            collective_id=0, has_side_effects=True, vmem_limit_bytes=53 << 20
        ),
        cost_estimate=pl.CostEstimate(flops=3 << 30, bytes_accessed=9 << 20, transcendentals=0),
        name="powers",
    )(vectors, self_blocks, dense)


def on_device_dense(
    vectors,
    slot_cluster,
    self_blocks,
    near_blocks,
    adjacent_group_couples,
    near_count,
    far_left,
    far_right,
    distant_group_couples,
    distant_active_number,
):
    local = vectors.shape[0]
    row_devices = lax.axis_size("row")
    col_devices = lax.axis_size("col")
    dense = build(
        local,
        local * col_devices,
        local * row_devices,
        slot_cluster,
        near_blocks,
        adjacent_group_couples,
        near_count,
        far_left,
        far_right,
        distant_group_couples,
        distant_active_number,
    )
    return powers(row_devices, col_devices, vectors, self_blocks, dense)


def on_device(
    vectors,
    slot_cluster,
    self_blocks,
    near_blocks,
    adjacent_group_couples,
    near_count,
    far_left,
    far_right,
    distant_group_couples,
    distant_active_number,
):
    local_slots = vectors.shape[0]
    row_devices = lax.axis_size("row")
    col_devices = lax.axis_size("col")
    row_span = local_slots * col_devices
    col_span = local_slots * row_devices
    grid_row = lax.axis_index("row")
    slot_ids = jnp.arange(slot_cluster.shape[0], dtype=jnp.int32)
    shape_tail = vectors.shape[1:]

    def locate(pairs):
        match = pairs[:, :, None] == slot_cluster[None, None, :]
        slots = jnp.sum(jnp.where(match, slot_ids[None, None, :], 0), axis=2)
        row_place = slots[:, 0] - grid_row * row_span
        owner = slots[:, 1] // local_slots
        col_place = owner // col_devices * local_slots + slots[:, 1] % local_slots
        return (row_place, col_place)

    def couple_activity(couple_number, coefficient_numbers):
        return (jnp.arange(coefficient_numbers, dtype=jnp.int32) < couple_number).astype(
            jnp.float32
        )[:, None, None]

    near_rows, near_cols = locate(adjacent_group_couples)
    far_rows, far_cols = locate(distant_group_couples)
    adjacent_active_markers = near_count[0]
    adjacent_couple_selector = couple_activity(
        adjacent_active_markers, adjacent_group_couples.shape[0]
    )
    distant_couple_selector = couple_activity(
        distant_active_number[0], distant_group_couples.shape[0]
    )
    current = vectors
    powers = []
    for step in range(ITERS):
        row_vectors = lax.all_gather(current, "col", axis=0, tiled=True)
        col_vectors = lax.all_gather(current, "row", axis=0, tiled=True)
        own_term = jnp.einsum(
            "cab,cnb->cna", self_blocks, current, preferred_element_type=jnp.float32
        )
        far_first = jnp.take(row_vectors, far_rows, axis=0)
        far_second = jnp.take(col_vectors, far_cols, axis=0)
        coef_fwd = jnp.einsum(
            "pkb,pnb->pnk", far_right, far_second, preferred_element_type=jnp.float32
        ).astype(jnp.bfloat16)
        coef_back = jnp.einsum(
            "pka,pna->pnk", far_left, far_first, preferred_element_type=jnp.float32
        ).astype(jnp.bfloat16)
        far_fwd = (
            jnp.einsum("pka,pnk->pna", far_left, coef_fwd, preferred_element_type=jnp.float32)
            * distant_couple_selector
        )
        far_back = (
            jnp.einsum("pkb,pnk->pnb", far_right, coef_back, preferred_element_type=jnp.float32)
            * distant_couple_selector
        )
        row_total = jnp.zeros((row_span,) + shape_tail, jnp.float32).at[far_rows].add(far_fwd)
        col_total = jnp.zeros((col_span,) + shape_tail, jnp.float32).at[far_cols].add(far_back)
        near_first = jnp.take(row_vectors, near_rows, axis=0)
        near_second = jnp.take(col_vectors, near_cols, axis=0)
        near_fwd = (
            jnp.einsum("pab,pnb->pna", near_blocks, near_second, preferred_element_type=jnp.float32)
            * adjacent_couple_selector
        )
        near_back = (
            jnp.einsum("pab,pna->pnb", near_blocks, near_first, preferred_element_type=jnp.float32)
            * adjacent_couple_selector
        )
        row_total = row_total.at[near_rows].add(near_fwd)
        col_total = col_total.at[near_cols].add(near_back)
        row_share = lax.psum_scatter(row_total, "col", scatter_dimension=0, tiled=True)
        col_share = lax.psum_scatter(col_total, "row", scatter_dimension=0, tiled=True)
        current = (own_term + row_share + col_share).astype(jnp.bfloat16)
        powers.append(current)
    return jnp.stack(powers)


def solution(mesh):
    def program(*args):
        leaf = args[0].shape[2]
        cells = args[0].shape[0] // mesh.shape["groups"]
        cells *= cells // (mesh.shape["row"] * mesh.shape["col"])
        fits = cells * leaf * leaf * 2 <= DENSE_LIMIT and mesh.shape["row"] == 4
        return mapped(mesh, on_device_dense if fits else on_device)(*args)

    return program


def mapped(mesh, body):
    return jax.shard_map(
        body,
        mesh=mesh,
        in_specs=(
            P(("groups", "row", "col"), None, None),
            P("groups"),
            P(("groups", "row", "col"), None, None),
            P(("groups", "row", "col"), None, None),
            P(("groups", "row", "col"), None),
            P(("groups", "row", "col")),
            P(("groups", "row", "col"), None, None),
            P(("groups", "row", "col"), None, None),
            P(("groups", "row", "col"), None),
            P(("groups", "row", "col")),
        ),
        out_specs=P(None, ("groups", "row", "col"), None, None),
        check_vma=False,
    )
```
